32 devices in a mesh: seq: 8 (over z, y), tp: 4 (over x, core).
Axes of the slice: x: 2, y: 2, z: 4, core: 2. Of those that a mesh axis runs over, the one named last changes fastest.
Arguments:
- tokens: bfloat16 [2048, 1280], P('seq', 'tp'), may hold values from -6 to 6
- first_gain: float32 [1280], replicated, may hold values from 0.1 to 1.9
- w_query: bfloat16 [1280, 1280], P(None, 'tp')
- w_key: bfloat16 [1280, 1280], P(None, 'tp')
- w_value: bfloat16 [1280, 1280], P(None, 'tp'), may hold values from -0.15625 to 0.15625
- w_out: bfloat16 [1280, 1280], P('tp'), may hold values from -0.625 to 0.625
- segment_ids: int32 [2048], P('seq'), may hold values from 0 to 11, never falling along the last dimension, each value on 1 to 512 neighbouring positions
- keep_mask: int32 [2048], P('seq'), may hold values 0 or 1
- merge_gain: float32 [1280], replicated, may hold values from 0.1 to 1.9
- w_merge: bfloat16 [5120, 640], P('tp'), may hold values from -0.078125 to 0.078125
- merge_index: int32 [512, 4], P('seq'), may hold values from 0 to 2047, as said below
- destination: int32 [512], P('seq'), may hold values from 0 to 511, as said below
Outputs:
- delivered: bfloat16 [512, 640], P('seq', 'tp')
The draws below stay inside these ranges and needn't reach their ends.
Inputs may be any that keep to these rules, and one draw needn't show every extreme that they name: `segment_ids`: segment numbers never fall along the tokens; each picture or clip holds 1 to 512 tokens and one holds exactly 512. `merge_index`: the four entries of merged row m are different tokens of the device that holds row m, that is of rows (m // 64) * 256 to that plus 256 - 1; every token lies in exactly one group. `destination`: a permutation of the merged rows. The owner of row m is destination[m] // 64; the 64 rows of each device go to exactly 8 owners, exactly 8 rows to each.
All inputs are finite; a program needn't handle non-finite values. No bound on the sum of `keep_mask` on one device may be relied on, other than what follows from the above.
Results may differ from the reference program's by a relative error of at most 0.022.
Values may be sent and summed in bfloat16 or wider, within the bound.
A program may use at most 64 MiB of HBM per device.

```python
import math
import jax
import jax.numpy as jnp
import numpy as np
from jax import lax

D = 1280
HEADS = 16
HD = 80
OUT = 640
TOK_DEV = 256
TOKENS = 2048
MROWS_DEV = 64
MTOT = 512
MOST = 512
COUNT = 12
CAP = 8
GROUPS_SENT = 8
N_SEQ = 8


def query_base(key):
    return jax.random.normal(jax.random.fold_in(key, 11), (D, D), jnp.float32) * D ** (-0.5)


def draw_w_query(key, part):
    return query_base(key).astype(jnp.bfloat16)


def draw_w_key(key, part):
    noise = jax.random.normal(jax.random.fold_in(key, 12), (D, D), jnp.float32) * D ** (-0.5)
    return noise.astype(jnp.bfloat16)


def shuffled(key, count, length):
    split_keys = jax.random.split(key, count)
    return jax.vmap(lambda sub_key: jax.random.permutation(sub_key, length))(split_keys).astype(jnp.int32)


def draw_merge_index(key, part):
    orders = shuffled(jax.random.fold_in(key, 21), N_SEQ, TOK_DEV)
    offsets = (jnp.arange(N_SEQ, dtype=jnp.int32) * TOK_DEV)[:, None]
    return (orders + offsets).reshape(MTOT, 4)


def draw_destination(key, part):
    first = jax.random.permutation(jax.random.fold_in(key, 31), N_SEQ).astype(jnp.int32)
    second = jax.random.permutation(jax.random.fold_in(key, 32), N_SEQ).astype(jnp.int32)
    shifts = jax.random.permutation(jax.random.fold_in(key, 33), N_SEQ).astype(jnp.int32)[:GROUPS_SENT]
    owners = first[(second[:, None] + shifts[None, :]) % N_SEQ]
    slot_orders = shuffled(jax.random.fold_in(key, 34), N_SEQ, MROWS_DEV)
    row_orders = shuffled(jax.random.fold_in(key, 35), N_SEQ, MROWS_DEV)
    within = jnp.arange(GROUPS_SENT, dtype=jnp.int32)[:, None] * CAP + jnp.arange(CAP, dtype=jnp.int32)[None, :]
    slots = slot_orders[owners[:, :, None], within[None, :, :]]
    targets = (owners[:, :, None] * MROWS_DEV + slots).reshape(N_SEQ, MROWS_DEV)
    result = jnp.zeros((N_SEQ, MROWS_DEV), jnp.int32)
    result = result.at[jnp.arange(N_SEQ, dtype=jnp.int32)[:, None], row_orders].set(targets)
    return result.reshape(MTOT)


def set_ends(drawn, rng, low, largest):
    longest = drawn.shape.index(max(drawn.shape))
    spots = []
    for shift in (0, 1):
        where = [jax.random.randint(jax.random.fold_in(rng, axis), (), 0, length) for axis, length in enumerate(drawn.shape)]
        where[longest] = (where[longest] + shift) % drawn.shape[longest]
        spots.append(tuple(where))
    return drawn.at[spots[0]].set(low).at[spots[1]].set(largest)


def block_levels(rng, extent, cuts, least, high):
    def one(dim, shards_of):
        draws = jax.random.uniform(jax.random.fold_in(jax.random.fold_in(rng, 6), dim), (shards_of,), jnp.float32, least / len(cuts), high / len(cuts))
        return jnp.repeat(jnp.exp(draws), extent[dim] // shards_of).reshape((-1,) + (1,) * (len(extent) - dim - 1))

    level = one(*cuts[0])
    for cut in cuts[1:]:
        level = level * one(*cut)
    return level


def split_up(amount, total, most, skew):
    portions = [(1 << 20) // math.isqrt(grade ** skew) + 1 for grade in range(2, amount + 1)]
    surplus, counts = total - most - (amount - 1), [1] * (amount - 1)
    while surplus > 0:
        candidates = [i for i in range(amount - 1) if counts[i] < most]
        whole, remaining = sum([portions[i] for i in candidates]), surplus
        for i in candidates:
            addition = min(most - counts[i], max(1, remaining * portions[i] // whole), surplus)
            counts[i] = counts[i] + addition
            surplus = surplus - addition
    return np.array([most] + counts)


def uneven_parts(key, count, total, most, slope):
    if count == 2:
        one = jax.random.randint(key, (), max(1, total - most), min(most, total - 1) + 1)
        return jnp.stack([one, total - one])
    tallies = jnp.asarray(split_up(count, total, most, slope), jnp.int32)
    couples = (count - 1) // 2
    giver, receiver = tallies[1:1 + 2 * couples:2], tallies[2:2 + 2 * couples:2]
    slack = jnp.minimum(giver - 1, most - receiver)
    moved = jax.random.randint(jax.random.fold_in(key, 1), (couples,), 0, 1 << 20) % (slack + 1)
    tallies = tallies.at[1:1 + 2 * couples:2].set(giver - moved).at[2:2 + 2 * couples:2].set(receiver + moved)
    return tallies[jax.random.permutation(jax.random.fold_in(key, 2), count)]


def centred(stream_key, extent, deviation, reach, shards=(), kind=jnp.bfloat16):
    drawn = jax.random.normal(stream_key, extent, jnp.float32) * deviation
    if len(shards) > 0:
        drawn = block_levels(stream_key, extent, shards, -0.22, 0.18) * drawn
    return jnp.clip(drawn, min=-reach, max=reach).astype(kind)


def setup_inputs(seed: int = 0) -> dict:
    streams_of = jax.random.split(jax.random.key(seed), 13)
    return {
        "tokens": centred(streams_of[0], (TOKENS, D), 1.0, 6.0, ((0, 8), (1, 4))),
        "first_gain": jnp.clip(1.0 + 0.18 * jax.random.normal(streams_of[1], (D,), jnp.float32), 0.1, 1.9),
        "w_query": draw_w_query(jax.random.fold_in(streams_of[12], 71), 0),
        "w_key": draw_w_key(jax.random.fold_in(streams_of[12], 71), 0),
        "w_value": centred(streams_of[4], (D, D), D ** -0.5, 0.15625, ((1, 4),)),
        "w_out": centred(streams_of[5], (D, D), HD ** -0.5, 0.625, ((0, 4),)),
        "segment_ids": jnp.searchsorted(jnp.cumsum(uneven_parts(streams_of[6], COUNT, TOKENS, MOST, 2)), jnp.arange(TOKENS), side="right").astype(jnp.int32),
        "keep_mask": set_ends((jax.random.randint(streams_of[7], (TOKENS,), 0, 8) < 7).astype(jnp.int32), jax.random.fold_in(streams_of[7], 1), 0, 1),
        "merge_gain": jnp.clip(1.0 + 0.18 * jax.random.normal(streams_of[8], (D,), jnp.float32), 0.1, 1.9),
        "w_merge": centred(streams_of[9], (4 * D, OUT), (4 * D) ** -0.5, 0.078125, ((0, 4),)),
        "merge_index": draw_merge_index(jax.random.fold_in(streams_of[12], 71), 0),
        "destination": draw_destination(jax.random.fold_in(streams_of[12], 71), 0),
    }


EPS = 1e-06

def layer_norm(activations, norm_gain):
    activations = activations.astype(jnp.float32)
    row_mean = lax.optimization_barrier(jnp.mean(activations, axis=-1, keepdims=True))
    centered = activations - row_mean
    variance = lax.optimization_barrier(jnp.mean(centered * centered, axis=-1, keepdims=True))
    return centered * lax.rsqrt(variance + EPS) * norm_gain.astype(jnp.float32)

def reference(tokens, first_gain, w_query, w_key, w_value, w_out, segment_ids, keep_mask, merge_gain, w_merge, merge_index, destination):
    normed = layer_norm(tokens, first_gain).astype(jnp.bfloat16)
    queries = jnp.dot(normed, w_query, preferred_element_type=jnp.float32).astype(jnp.bfloat16)
    key_rows = jnp.dot(normed, w_key, preferred_element_type=jnp.float32).astype(jnp.bfloat16)
    value_rows = jnp.dot(normed, w_value, preferred_element_type=jnp.float32).astype(jnp.bfloat16)
    code_query = segment_ids + 1
    code_key = jnp.where(keep_mask > 0, segment_ids + 1, 0)
    margin = 2 * TOK_DEV
    key_padded = jnp.pad(key_rows, ((margin, margin), (0, 0)))
    value_padded = jnp.pad(value_rows, ((margin, margin), (0, 0)))
    code_padded = jnp.pad(code_key, ((margin, margin),))
    score_scale = HD ** (-0.5)
    window = 5 * TOK_DEV

    def attend_block(block_index):
        block_start = (block_index * TOK_DEV).astype(jnp.int32)
        query_block = lax.dynamic_slice_in_dim(queries, block_start, TOK_DEV, 0)
        key_block = lax.dynamic_slice_in_dim(key_padded, block_start, window, 0)
        value_block = lax.dynamic_slice_in_dim(value_padded, block_start, window, 0)
        query_codes = lax.dynamic_slice_in_dim(code_query, block_start, TOK_DEV, 0)
        key_codes = lax.dynamic_slice_in_dim(code_padded, block_start, window, 0)
        query_pos = jnp.arange(TOK_DEV)[:, None]
        key_pos = jnp.arange(window)[None, :]
        allowed = (query_codes[:, None] == key_codes[None, :]) | (key_pos == query_pos + margin)
        query_heads = query_block.reshape(TOK_DEV, HEADS, HD).astype(jnp.float32)
        key_heads = key_block.reshape(window, HEADS, HD).astype(jnp.float32)
        value_heads = value_block.reshape(window, HEADS, HD).astype(jnp.float32)
        scores = jnp.einsum('qhd,khd->hqk', query_heads, key_heads) * score_scale
        scores = jnp.where(allowed[None], scores, -1e+30)
        row_max = lax.optimization_barrier(jnp.max(scores, axis=-1, keepdims=True))
        exponent = jnp.exp(scores - row_max)
        row_total = lax.optimization_barrier(jnp.sum(exponent, axis=-1, keepdims=True))
        weights = (exponent / row_total).astype(jnp.bfloat16)
        result = jnp.einsum('hqk,khd->qhd', weights.astype(jnp.float32), value_heads)
        return result.reshape(TOK_DEV, D).astype(jnp.bfloat16)
    attended = lax.map(attend_block, jnp.arange(N_SEQ, dtype=jnp.int32)).reshape(TOKENS, D)
    mixed_sum = jnp.dot(attended, w_out, preferred_element_type=jnp.float32)
    updated = tokens.astype(jnp.float32) + mixed_sum
    merged_norm = layer_norm(updated, merge_gain).astype(jnp.bfloat16)
    grouped = jnp.take(merged_norm, merge_index, axis=0).reshape(MTOT, 4 * D)
    projected = jnp.dot(grouped, w_merge, preferred_element_type=jnp.float32).astype(jnp.bfloat16)
    delivered = jnp.zeros((MTOT, OUT), jnp.bfloat16).at[destination].set(projected)
    return delivered
```

```python
import functools

import jax
import jax.numpy as jnp
from jax import lax
from jax.experimental import pallas as pl
from jax.experimental.pallas import tpu as pltpu
from jax.sharding import PartitionSpec as P

HD = 80
EPS = 1e-06
LOG2E = 1.4426950408889634
MESH = pl.DeviceIdType.MESH
OFFSETS = (1, -1, 2, -2)
KEY_WINDOW = (0, 0, 128, 128)
VALUE_WINDOW = (256, 256, 384, 384)
F32 = jnp.float32
BF16 = jnp.bfloat16


def normalise(rows, gain):
    mean = jnp.mean(rows, axis=-1, keepdims=True)
    centered = rows - mean
    variance = jnp.mean(centered * centered, axis=-1, keepdims=True)
    return centered * lax.rsqrt(variance + EPS) * gain


def kernel(
    n, tp,
    tokens, first_gain, w_query, w_key, w_value, w_out, segments, keep,
    merge_gain, w_merge, merge_index, destination,
    out,
    gathered, wq, wk, wv, wo, wm, pairs, codes, dests, queries,
    part_send, part_recv, proj_send, proj_recv, rows,
    local_sem, tok_send, tok_recv, pair_send, pair_recv, code_send, code_recv,
    dest_send, dest_recv, part_ssem, part_rsem, proj_ssem, proj_rsem, row_send, row_recv,
):
    s, t = lax.axis_index("seq"), lax.axis_index("tp")
    count = tokens.shape[0]
    width = tokens.shape[1]
    merged = merge_index.shape[0]

    barrier = pltpu.get_barrier_semaphore()
    for d in range(1, tp):
        pl.semaphore_signal(barrier, inc=1, device_id=(s, lax.rem(t + d, tp)), device_id_type=MESH)

    @pl.loop(1, n)
    def _(d):
        pl.semaphore_signal(barrier, inc=1, device_id=(lax.rem(s + d, n), t), device_id_type=MESH)

    half = w_out.shape[0] // 2
    local = [
        pltpu.make_async_copy(tokens, gathered.at[t], local_sem.at[0]),
        pltpu.make_async_copy(w_key, wk, local_sem.at[1]),
        pltpu.make_async_copy(w_value, wv, local_sem.at[2]),
        pltpu.make_async_copy(w_query, wq, local_sem.at[3]),
        pltpu.make_async_copy(w_out.at[pl.ds(0, half)], wo.at[pl.ds(64, half)], local_sem.at[4]),
        pltpu.make_async_copy(w_out.at[pl.ds(half, half)], wo.at[pl.ds(352, half)], local_sem.at[5]),
        pltpu.make_async_copy(w_merge, wm, local_sem.at[6]),
    ]
    for copy in local:
        copy.start()
    wo[0:64, :] = jnp.zeros((64, wo.shape[1]), BF16)
    wo[224:352, :] = jnp.zeros((128, wo.shape[1]), BF16)
    code_query = segments[...] + 1
    codes[0] = jnp.where(keep[...] > 0, code_query, 0)
    dests[s] = destination[...]

    pl.semaphore_wait(barrier, tp - 1 + n - 1)

    def tok_copy(d):
        return pltpu.make_async_remote_copy(
            src_ref=tokens, dst_ref=gathered.at[t],
            send_sem=tok_send.at[d], recv_sem=tok_recv.at[d],
            device_id=(s, lax.rem(t + d, tp)), device_id_type=MESH)

    for d in range(1, tp):
        tok_copy(d).start()

    def code_copy(i):
        return pltpu.make_async_remote_copy(
            src_ref=codes.at[0], dst_ref=codes.at[i + 1],
            send_sem=code_send.at[i], recv_sem=code_recv.at[i],
            device_id=(s + OFFSETS[i], t), device_id_type=MESH)

    def pair_copy(i):
        return pltpu.make_async_remote_copy(
            src_ref=pairs.at[0], dst_ref=pairs.at[i + 1],
            send_sem=pair_send.at[i], recv_sem=pair_recv.at[i],
            device_id=(s + OFFSETS[i], t), device_id_type=MESH)

    def has(offset):
        return (s + offset >= 0) & (s + offset < n)

    for i, o in enumerate(OFFSETS):
        @pl.when(has(o))
        def _():
            code_copy(i).start()

    def dest_copy(d):
        return pltpu.make_async_remote_copy(
            src_ref=dests.at[s], dst_ref=dests.at[s],
            send_sem=dest_send.at[d], recv_sem=dest_recv.at[d],
            device_id=(lax.rem(s + d, n), t), device_id_type=MESH)

    @pl.loop(1, n)
    def _(d):
        dest_copy(d).start()

    for i, o in enumerate(OFFSETS):
        @pl.when(jnp.logical_not(has(-o)))
        def _():
            pairs[i + 1] = jnp.zeros(pairs.shape[1:], BF16)
            codes[i + 1] = jnp.zeros(codes.shape[1:], jnp.int32)

    token_lane = lax.broadcasted_iota(jnp.int32, (merged, count), 1)
    index = merge_index[...] - s * count
    picks = [(index[:, j:j + 1] == token_lane).astype(BF16) for j in range(tp)]
    pick_all = jnp.concatenate(picks, axis=0)
    pos_lane = lax.broadcasted_iota(jnp.int32, index.shape, 1)
    mine = jnp.sum(jnp.where(pos_lane == t, index, 0), axis=1, keepdims=True)
    pick_mine = (mine == token_lane).astype(BF16)
    diag = lax.broadcasted_iota(jnp.int32, (count, count), 0) == lax.broadcasted_iota(jnp.int32, (count, count), 1)
    code_column = jnp.sum(jnp.where(diag, code_query, 0), axis=1, keepdims=True)

    for d in range(1, tp):
        tok_copy(d).wait_recv()
    local[0].wait()
    whole = jnp.concatenate([gathered[j].astype(F32) for j in range(tp)], axis=1)
    residual = jnp.dot(pick_mine, whole.astype(BF16), preferred_element_type=F32)
    normed = normalise(whole, first_gain[...]).astype(BF16)
    local[1].wait()
    local[2].wait()
    pairs[0] = jnp.concatenate(
        [jnp.dot(normed, wk[...], preferred_element_type=F32),
         jnp.dot(normed, wv[...], preferred_element_type=F32)], axis=1).astype(BF16)
    for i, o in enumerate(OFFSETS):
        @pl.when(has(o))
        def _():
            pair_copy(i).start()

    local[3].wait()
    q = jnp.dot(normed, wq[...], preferred_element_type=F32)
    queries[...] = jnp.concatenate([q, jnp.zeros((count, 64), F32)], axis=1).astype(BF16)
    lane = lax.broadcasted_iota(jnp.int32, (count, 256), 1)
    head_q = []
    for h in range(4):
        start = KEY_WINDOW[h]
        inside = (lane + start >= h * HD) & (lane + start < (h + 1) * HD)
        head_q.append(jnp.where(inside, queries[:, start:start + 256], jnp.zeros((), BF16)))

    factor = HD ** (-0.5) * LOG2E
    state = [None] * 4
    for b in range(5):
        if b:
            i = b - 1

            @pl.when(has(-OFFSETS[i]))
            def _():
                code_copy(i).wait_recv()
                pair_copy(i).wait_recv()
        allowed = code_column == codes[b]
        if b == 0:
            allowed = allowed | diag
        for h in range(4):
            key = pairs[b, :, KEY_WINDOW[h]:KEY_WINDOW[h] + 256]
            value = pairs[b, :, VALUE_WINDOW[h]:VALUE_WINDOW[h] + 256]
            scores = lax.dot_general(head_q[h], key, (((1,), (1,)), ((), ())), preferred_element_type=F32)
            scores = jnp.where(allowed, scores * factor, -1e30)
            top = jnp.max(scores, axis=1, keepdims=True)
            if b:
                top = jnp.maximum(top, state[h][0])
            expo = jnp.exp2(scores - top)
            total = jnp.sum(expo, axis=1, keepdims=True)
            acc = jnp.dot(expo.astype(BF16), value, preferred_element_type=F32)
            if b:
                shrink = jnp.exp2(state[h][0] - top)
                total = total + shrink * state[h][1]
                acc = acc + shrink * state[h][2]
            state[h] = (top, total, acc)

    heads = [acc / total for _, total, acc in state]
    attended = jnp.concatenate(
        [jnp.where(lane < 144, heads[0], heads[1]), jnp.where(lane < 176, heads[2], heads[3])],
        axis=1).astype(BF16)
    attended = jnp.dot(pick_all, attended, preferred_element_type=F32).astype(BF16)
    local[4].wait()
    local[5].wait()

    def part_copy(d):
        peer = lax.rem(t + d, tp)
        return pltpu.make_async_remote_copy(
            src_ref=part_send.at[peer], dst_ref=part_recv.at[d],
            send_sem=part_ssem.at[d], recv_sem=part_rsem.at[d],
            device_id=(s, peer), device_id_type=MESH)

    part = jnp.dot(attended, wo[...], preferred_element_type=F32).astype(BF16)
    for j in range(tp):
        part_send[j] = part[j * merged:(j + 1) * merged]
    for d in range(1, tp):
        part_copy(d).start()
    updated = residual + part_send[t].astype(F32)
    for d in range(1, tp):
        part_copy(d).wait_recv()
        updated = updated + part_recv[d].astype(F32)
    merged_norm = normalise(updated, merge_gain[...]).astype(BF16)
    local[6].wait()
    proj = jnp.dot(merged_norm, wm[...], preferred_element_type=F32)
    piece = proj.shape[1] // tp
    for j in range(tp):
        proj_send[j] = proj[:, j * piece:(j + 1) * piece].astype(BF16)

    def proj_copy(d):
        peer = lax.rem(t + d, tp)
        return pltpu.make_async_remote_copy(
            src_ref=proj_send.at[peer], dst_ref=proj_recv.at[d],
            send_sem=proj_ssem.at[d], recv_sem=proj_rsem.at[d],
            device_id=(s, peer), device_id_type=MESH)

    for d in range(1, tp):
        proj_copy(d).start()
    projected = proj_send[t].astype(F32)
    for d in range(1, tp):
        proj_copy(d).wait_recv()
        projected = projected + proj_recv[d].astype(F32)
    rows[s] = projected.astype(BF16)

    def row_copy(d):
        return pltpu.make_async_remote_copy(
            src_ref=rows.at[s], dst_ref=rows.at[s],
            send_sem=row_send.at[d], recv_sem=row_recv.at[d],
            device_id=(lax.rem(s + d, n), t), device_id_type=MESH)

    @pl.loop(1, n)
    def _(d):
        row_copy(d).start()

    slot = lax.broadcasted_iota(jnp.int32, (merged, merged), 0)

    def deliver(source):
        one_hot = ((dests[source] - s * merged) == slot).astype(BF16)
        return jnp.dot(one_hot, rows[source], preferred_element_type=F32)

    def step(d, total):
        dest_copy(d).wait_recv()
        row_copy(d).wait_recv()
        return total + deliver(lax.rem(s + n - d, n))

    total = lax.fori_loop(1, n, step, deliver(s))
    out[...] = total.astype(BF16)

    for d in range(1, tp):
        tok_copy(d).wait_send()
        part_copy(d).wait_send()
        proj_copy(d).wait_send()
    for i, o in enumerate(OFFSETS):
        @pl.when(has(o))
        def _():
            code_copy(i).wait_send()
            pair_copy(i).wait_send()

    @pl.loop(1, n)
    def _(d):
        dest_copy(d).wait_send()
        row_copy(d).wait_send()


def body(n, tp, tokens, first_gain, w_query, w_key, w_value, w_out, segment_ids, keep_mask,
         merge_gain, w_merge, merge_index, destination):
    count, width = tokens.shape
    features = w_query.shape[0]
    merged = merge_index.shape[0]
    piece = w_merge.shape[1] // tp
    anywhere = pl.BlockSpec(memory_space=pl.ANY)
    vmem = pl.BlockSpec(memory_space=pltpu.VMEM)
    dma = pltpu.SemaphoreType.DMA
    return pl.pallas_call(
        functools.partial(kernel, n, tp),
        out_shape=jax.ShapeDtypeStruct((merged, piece), BF16),
        in_specs=[anywhere, vmem, anywhere, anywhere, anywhere, anywhere, vmem, vmem, vmem, anywhere, vmem, vmem],
        out_specs=vmem,
        scratch_shapes=[
            pltpu.VMEM((tp, count, width), BF16),
            pltpu.VMEM(w_query.shape, BF16),
            pltpu.VMEM(w_key.shape, BF16),
            pltpu.VMEM(w_value.shape, BF16),
            pltpu.VMEM((512, features), BF16),
            pltpu.VMEM(w_merge.shape, BF16),
            pltpu.VMEM((5, count, 2 * width), BF16),
            pltpu.VMEM((5, 1, count), jnp.int32),
            pltpu.VMEM((n, 1, merged), jnp.int32),
            pltpu.VMEM((count, 384), BF16),
            pltpu.VMEM((tp, merged, features), BF16),
            pltpu.VMEM((tp, merged, features), BF16),
            pltpu.VMEM((tp, merged, piece), BF16),
            pltpu.VMEM((tp, merged, piece), BF16),
            pltpu.VMEM((n, merged, piece), BF16),
            dma((7,)),
            dma((tp,)), dma((tp,)),
            dma((4,)), dma((4,)), dma((4,)), dma((4,)),
            dma((n,)), dma((n,)),
            dma((tp,)), dma((tp,)), dma((tp,)), dma((tp,)),
            dma((n,)), dma((n,)),
        ],
        compiler_params=pltpu.CompilerParams(
            collective_id=0, has_side_effects=True, vmem_limit_bytes=56 * 1024 * 1024),
        name="vision_layer",
    )(tokens, first_gain.reshape(1, -1), w_query, w_key, w_value, w_out,
      segment_ids.reshape(1, -1), keep_mask.reshape(1, -1), merge_gain.reshape(1, -1),
      w_merge, merge_index, destination.reshape(1, -1))


def solution(mesh):
    n, tp = mesh.shape["seq"], mesh.shape["tp"]
    return jax.shard_map(
        functools.partial(body, n, tp),
        mesh=mesh,
        in_specs=(
            P("seq", "tp"), P(), P(None, "tp"), P(None, "tp"), P(None, "tp"), P("tp", None),
            P("seq"), P("seq"), P(), P("tp", None), P("seq", None), P("seq"),
        ),
        out_specs=P("seq", "tp"),
        check_vma=False,
    )
```

```python
import functools

import jax
import jax.numpy as jnp
from jax import lax
from jax.experimental import pallas as pl
from jax.experimental.pallas import tpu as pltpu
from jax.sharding import PartitionSpec as P

HD = 80
EPS = 1e-06
LOG2E = 1.4426950408889634
MESH = pl.DeviceIdType.MESH
OFFSETS = (1, -1, 2, -2)
F32 = jnp.float32
BF16 = jnp.bfloat16


def normalise(rows, gain, axis):
    mean = jnp.mean(rows, axis=axis, keepdims=True)
    centered = rows - mean
    variance = jnp.mean(centered * centered, axis=axis, keepdims=True)
    return centered * lax.rsqrt(variance + EPS) * gain


def kernel(
    n, tp,
    tokens, first_gain, w_query, w_key, w_value, w_out, segments, keep,
    merge_gain, w_merge, merge_index, destination,
    out,
    gathered, wq, wk, wv, wo, wm, pairs, codes, dests, queries,
    picks, part_send, part_recv, proj_send, proj_recv, rows,
    local_sem, tok_send, tok_recv, pair_send, pair_recv, code_send, code_recv,
    dest_send, dest_recv, part_ssem, part_rsem, proj_ssem, proj_rsem, row_send, row_recv,
):
    s, t = lax.axis_index("seq"), lax.axis_index("tp")
    width, count = tokens.shape
    merged = merge_index.shape[1]
    beside, across, far = t + 1 - 2 * lax.rem(t, 2), lax.rem(t + 2, 4), 3 - t

    barrier = pltpu.get_barrier_semaphore()
    for d in range(1, tp):
        pl.semaphore_signal(barrier, inc=1, device_id=(s, lax.rem(t + d, tp)), device_id_type=MESH)

    @pl.loop(1, n)
    def _(d):
        pl.semaphore_signal(barrier, inc=1, device_id=(lax.rem(s + d, n), t), device_id_type=MESH)

    local = [
        pltpu.make_async_copy(tokens, gathered.at[t], local_sem.at[0]),
        pltpu.make_async_copy(w_key, wk, local_sem.at[1]),
        pltpu.make_async_copy(w_value, wv, local_sem.at[2]),
        pltpu.make_async_copy(w_query, wq, local_sem.at[3]),
        pltpu.make_async_copy(w_out, wo, local_sem.at[4]),
        pltpu.make_async_copy(w_merge, wm, local_sem.at[5]),
    ]
    for copy in local:
        copy.start()
    code_query = segments[...] + 1
    codes[0] = jnp.where(keep[...] > 0, code_query, 0)
    dests[s] = destination[...]

    pl.semaphore_wait(barrier, tp - 1 + n - 1)

    half = width // 2

    def tok_copy(i):
        if i == 2:
            source, target, peer = tokens, gathered.at[t], beside
        elif i < 2:
            part = pl.ds(i * half, half)
            source, target, peer = tokens.at[part], gathered.at[t, part], across
        else:
            part = pl.ds((i - 3) * half, half)
            source = gathered.at[across, part]
            target, peer = source, beside
        return pltpu.make_async_remote_copy(
            src_ref=source, dst_ref=target, send_sem=tok_send.at[i], recv_sem=tok_recv.at[i],
            device_id=(s, peer), device_id_type=MESH)

    for i in range(3):
        tok_copy(i).start()

    def code_copy(i):
        return pltpu.make_async_remote_copy(
            src_ref=codes.at[0], dst_ref=codes.at[i + 1],
            send_sem=code_send.at[i], recv_sem=code_recv.at[i],
            device_id=(s + OFFSETS[i], t), device_id_type=MESH)

    def pair_copy(i):
        return pltpu.make_async_remote_copy(
            src_ref=pairs.at[0], dst_ref=pairs.at[i + 1],
            send_sem=pair_send.at[i], recv_sem=pair_recv.at[i],
            device_id=(s + OFFSETS[i], t), device_id_type=MESH)

    def has(offset):
        return (s + offset >= 0) & (s + offset < n)

    for i, o in enumerate(OFFSETS):
        @pl.when(has(o))
        def _():
            code_copy(i).start()

    def dest_copy(d):
        return pltpu.make_async_remote_copy(
            src_ref=dests.at[s], dst_ref=dests.at[s],
            send_sem=dest_send.at[d], recv_sem=dest_recv.at[d],
            device_id=(lax.rem(s + d, n), t), device_id_type=MESH)

    @pl.loop(1, n)
    def _(d):
        dest_copy(d).start()

    for i, o in enumerate(OFFSETS):
        @pl.when(jnp.logical_not(has(-o)))
        def _():
            pairs[i + 1] = jnp.zeros(pairs.shape[1:], BF16)
            codes[i + 1] = jnp.zeros(codes.shape[1:], jnp.int32)

    index = merge_index[...] - s * count
    order = jnp.concatenate([index[j:j + 1] for j in range(tp)], axis=1)
    square = (count, count)
    down = lax.broadcasted_iota(jnp.int32, square, 0)
    along = lax.broadcasted_iota(jnp.int32, square, 1)
    diag = down == along
    order_column = jnp.sum(jnp.where(diag, order, 0), axis=1, keepdims=True)
    pick_all = (order_column == along).astype(BF16)
    picks[...] = pick_all

    def column(row):
        return jnp.sum(jnp.where(diag, row, 0), axis=1, keepdims=True)

    gain = first_gain[...].reshape(1, -1)
    gain_column = jnp.transpose(jnp.broadcast_to(gain, (128, gain.shape[1])))[:, 0:1]

    for i in range(2):
        tok_copy(i).wait_recv()
        tok_copy(i + 3).start()
    local[0].wait()
    tok_copy(2).wait_recv()
    for i in range(2):
        tok_copy(i + 3).wait_recv()
    packed = gathered[...].reshape(tp * width, count)
    residual = lax.dot_general(
        picks[pl.ds(pl.multiple_of(t * merged, merged), merged), :], packed,
        (((1,), (1,)), ((), ())), preferred_element_type=F32)
    normed = normalise(packed.astype(F32), gain_column, 0).astype(BF16)
    local[1].wait()
    pairs[0, 0:width] = jnp.dot(wk[...], normed, preferred_element_type=F32).astype(BF16)
    local[2].wait()
    pairs[0, width:2 * width] = jnp.dot(wv[...], normed, preferred_element_type=F32).astype(BF16)
    for i, o in enumerate(OFFSETS):
        @pl.when(has(o))
        def _():
            pair_copy(i).start()

    local[3].wait()
    queries[...] = jnp.dot(wq[...], normed, preferred_element_type=F32).astype(BF16)

    factor = HD ** (-0.5) * LOG2E
    state = [None] * 4
    for b in range(5):
        if b:
            i = b - 1

            @pl.when(has(-OFFSETS[i]))
            def _():
                code_copy(i).wait_recv()
                pair_copy(i).wait_recv()
        allowed = column(codes[b]) == code_query
        if b == 0:
            allowed = allowed | diag
        for h in range(4):
            key = pairs[b, h * HD:(h + 1) * HD]
            value = pairs[b, width + h * HD:width + (h + 1) * HD]
            scores = lax.dot_general(
                key, queries[h * HD:(h + 1) * HD], (((0,), (0,)), ((), ())), preferred_element_type=F32)
            scores = jnp.where(allowed, scores * factor, -1e30)
            top = jnp.max(scores, axis=0, keepdims=True)
            if b:
                top = jnp.maximum(top, state[h][0])
            expo = jnp.exp2(scores - top)
            total = jnp.sum(expo, axis=0, keepdims=True)
            acc = jnp.dot(value, expo.astype(BF16), preferred_element_type=F32)
            if b:
                shrink = jnp.exp2(state[h][0] - top)
                total = total + shrink * state[h][1]
                acc = acc + shrink * state[h][2]
            state[h] = (top, total, acc)

    attended = jnp.concatenate([acc / total for _, total, acc in state], axis=0).astype(BF16)
    attended = lax.dot_general(
        picks[...], attended, (((1,), (1,)), ((), ())), preferred_element_type=F32).astype(BF16)
    local[4].wait()

    def part_copy(i):
        source = part_send.at[(far, beside, across)[i]]
        return pltpu.make_async_remote_copy(
            src_ref=source, dst_ref=part_recv.at[i], send_sem=part_ssem.at[i], recv_sem=part_rsem.at[i],
            device_id=(s, (beside, beside, across)[i]), device_id_type=MESH)

    part = jnp.dot(attended, wo[...], preferred_element_type=F32).astype(BF16)
    for j in range(tp):
        part_send[j] = part[j * merged:(j + 1) * merged]
    part_copy(0).start()
    part_copy(1).start()
    part_copy(0).wait_recv()
    part_send[across] = (part_send[across].astype(F32) + part_recv[0].astype(F32)).astype(BF16)
    part_copy(2).start()
    part_copy(1).wait_recv()
    updated = residual + part_send[t].astype(F32) + part_recv[1].astype(F32)
    part_copy(2).wait_recv()
    updated = updated + part_recv[2].astype(F32)
    merged_norm = normalise(updated, merge_gain[...].reshape(1, -1), 1).astype(BF16)
    local[5].wait()
    proj = jnp.dot(merged_norm, wm[...], preferred_element_type=F32)
    piece = proj.shape[1] // tp
    for j in range(tp):
        proj_send[j] = proj[:, j * piece:(j + 1) * piece].astype(BF16)

    def proj_copy(d):
        peer = lax.rem(t + d, tp)
        return pltpu.make_async_remote_copy(
            src_ref=proj_send.at[peer], dst_ref=proj_recv.at[d],
            send_sem=proj_ssem.at[d], recv_sem=proj_rsem.at[d],
            device_id=(s, peer), device_id_type=MESH)

    for d in range(1, tp):
        proj_copy(d).start()
    projected = proj_send[t].astype(F32)
    for d in range(1, tp):
        proj_copy(d).wait_recv()
        projected = projected + proj_recv[d].astype(F32)
    rows[s] = projected.astype(BF16)

    def row_copy(d):
        return pltpu.make_async_remote_copy(
            src_ref=rows.at[s], dst_ref=rows.at[s],
            send_sem=row_send.at[d], recv_sem=row_recv.at[d],
            device_id=(lax.rem(s + d, n), t), device_id_type=MESH)

    @pl.loop(1, n)
    def _(d):
        row_copy(d).start()

    slot = lax.broadcasted_iota(jnp.int32, (merged, merged), 0)

    def deliver(source):
        one_hot = ((dests[source] - s * merged) == slot).astype(BF16)
        return jnp.dot(one_hot, rows[source], preferred_element_type=F32)

    def step(d, total):
        dest_copy(d).wait_recv()
        row_copy(d).wait_recv()
        return total + deliver(lax.rem(s + n - d, n))

    total = lax.fori_loop(1, n, step, deliver(s))
    out[...] = total.astype(BF16)

    for i in range(5):
        tok_copy(i).wait_send()
    for i in range(3):
        part_copy(i).wait_send()
    for d in range(1, tp):
        proj_copy(d).wait_send()
    for i, o in enumerate(OFFSETS):
        @pl.when(has(o))
        def _():
            code_copy(i).wait_send()
            pair_copy(i).wait_send()

    @pl.loop(1, n)
    def _(d):
        dest_copy(d).wait_send()
        row_copy(d).wait_send()


def body(n, tp, tokens, first_gain, w_query, w_key, w_value, w_out, segment_ids, keep_mask,
         merge_gain, w_merge, merge_index, destination):
    count, width = tokens.shape
    features = w_query.shape[0]
    merged = merge_index.shape[0]
    piece = w_merge.shape[1] // tp
    anywhere = pl.BlockSpec(memory_space=pl.ANY)
    vmem = pl.BlockSpec(memory_space=pltpu.VMEM)
    dma = pltpu.SemaphoreType.DMA
    return pl.pallas_call(
        functools.partial(kernel, n, tp),
        out_shape=jax.ShapeDtypeStruct((merged, piece), BF16),
        in_specs=[anywhere, vmem, anywhere, anywhere, anywhere, anywhere, vmem, vmem, vmem, anywhere, vmem, vmem],
        out_specs=vmem,
        scratch_shapes=[
            pltpu.VMEM((tp, width, count), BF16),
            pltpu.VMEM(w_query.shape[::-1], BF16),
            pltpu.VMEM(w_key.shape[::-1], BF16),
            pltpu.VMEM(w_value.shape[::-1], BF16),
            pltpu.VMEM(w_out.shape, BF16),
            pltpu.VMEM(w_merge.shape, BF16),
            pltpu.VMEM((5, 2 * width, count), BF16),
            pltpu.VMEM((5, 1, count), jnp.int32),
            pltpu.VMEM((n, 1, merged), jnp.int32),
            pltpu.VMEM((width, count), BF16),
            pltpu.VMEM((count, count), BF16),
            pltpu.VMEM((tp, merged, features), BF16),
            pltpu.VMEM((tp, merged, features), BF16),
            pltpu.VMEM((tp, merged, piece), BF16),
            pltpu.VMEM((tp, merged, piece), BF16),
            pltpu.VMEM((n, merged, piece), BF16),
            dma((6,)),
            dma((5,)), dma((5,)),
            dma((4,)), dma((4,)), dma((4,)), dma((4,)),
            dma((n,)), dma((n,)),
            dma((tp,)), dma((tp,)), dma((tp,)), dma((tp,)),
            dma((n,)), dma((n,)),
        ],
        compiler_params=pltpu.CompilerParams(
            collective_id=0, has_side_effects=True, vmem_limit_bytes=56 * 1024 * 1024),
        name="vision_layer",
    )(tokens.T, first_gain, w_query.T, w_key.T, w_value.T, w_out,
      segment_ids.reshape(1, -1), keep_mask.reshape(1, -1), merge_gain,
      w_merge, merge_index.T, destination.reshape(1, -1))


def solution(mesh):
    n, tp = mesh.shape["seq"], mesh.shape["tp"]
    return jax.shard_map(
        functools.partial(body, n, tp),
        mesh=mesh,
        in_specs=(
            P("seq", "tp"), P(), P(None, "tp"), P(None, "tp"), P(None, "tp"), P("tp", None),
            P("seq"), P("seq"), P(), P("tp", None), P("seq", None), P("seq"),
        ),
        out_specs=P("seq", "tp"),
        check_vma=False,
    )
```

```python
import functools

import jax
import jax.numpy as jnp
from jax import lax
from jax.experimental import pallas as pl
from jax.experimental.pallas import tpu as pltpu
from jax.sharding import PartitionSpec as P

HD = 80
EPS = 1e-06
LOG2E = 1.4426950408889634
MESH = pl.DeviceIdType.MESH
BLOCK = 16
OFFSETS = (1, -1, 2, -2)
F32 = jnp.float32
BF16 = jnp.bfloat16


def normalise(rows, gain, axis):
    mean = jnp.mean(rows, axis=axis, keepdims=True)
    centered = rows - mean
    variance = jnp.mean(centered * centered, axis=axis, keepdims=True)
    return centered * lax.rsqrt(variance + EPS) * gain


def kernel(
    n, tp,
    tokens, first_gain, w_query, w_key, w_value, w_out, segments, keep,
    merge_gain, w_merge, merge_index, destination,
    out,
    gathered, wq, wk, wv, wo, wm, pairs, codes, dests, queries,
    picks, part_send, part_recv, proj_send, proj_recv, sort, spread, leaving, rows,
    local_sem, tok_send, tok_recv, pair_send, pair_recv, code_send, code_recv,
    dest_send, dest_recv, part_ssem, part_rsem, proj_ssem, proj_rsem, row_send, row_recv,
):
    s, t = lax.axis_index("seq"), lax.axis_index("tp")
    width, count = tokens.shape
    merged = merge_index.shape[1]
    beside, across, far = t + 1 - 2 * lax.rem(t, 2), lax.rem(t + 2, 4), 3 - t

    barrier = pltpu.get_barrier_semaphore()
    for d in range(1, tp):
        pl.semaphore_signal(barrier, inc=1, device_id=(s, lax.rem(t + d, tp)), device_id_type=MESH)

    @pl.loop(1, n)
    def _(d):
        pl.semaphore_signal(barrier, inc=1, device_id=(lax.rem(s + d, n), t), device_id_type=MESH)

    local = [
        pltpu.make_async_copy(tokens, gathered.at[t], local_sem.at[0]),
        pltpu.make_async_copy(w_key, wk, local_sem.at[1]),
        pltpu.make_async_copy(w_value, wv, local_sem.at[2]),
        pltpu.make_async_copy(w_query, wq, local_sem.at[3]),
        pltpu.make_async_copy(w_out, wo, local_sem.at[4]),
        pltpu.make_async_copy(w_merge, wm, local_sem.at[5]),
    ]
    for copy in local:
        copy.start()
    code_query = segments[...] + 1
    codes[0] = jnp.where(keep[...] > 0, code_query, 0)
    dests[s] = destination[...]

    pl.semaphore_wait(barrier, tp - 1 + n - 1)

    half = width // 2

    def tok_copy(i):
        if i == 2:
            source, target, peer = tokens, gathered.at[t], beside
        elif i < 2:
            part = pl.ds(i * half, half)
            source, target, peer = tokens.at[part], gathered.at[t, part], across
        else:
            part = pl.ds((i - 3) * half, half)
            source = gathered.at[across, part]
            target, peer = source, beside
        return pltpu.make_async_remote_copy(
            src_ref=source, dst_ref=target, send_sem=tok_send.at[i], recv_sem=tok_recv.at[i],
            device_id=(s, peer), device_id_type=MESH)

    for i in range(3):
        tok_copy(i).start()

    def code_copy(i):
        return pltpu.make_async_remote_copy(
            src_ref=codes.at[0], dst_ref=codes.at[i + 1],
            send_sem=code_send.at[i], recv_sem=code_recv.at[i],
            device_id=(s + OFFSETS[i], t), device_id_type=MESH)

    def pair_copy(i):
        return pltpu.make_async_remote_copy(
            src_ref=pairs.at[0], dst_ref=pairs.at[i + 1],
            send_sem=pair_send.at[i], recv_sem=pair_recv.at[i],
            device_id=(s + OFFSETS[i], t), device_id_type=MESH)

    def has(offset):
        return (s + offset >= 0) & (s + offset < n)

    for i, o in enumerate(OFFSETS):
        @pl.when(has(o))
        def _():
            code_copy(i).start()

    def dest_copy(d):
        return pltpu.make_async_remote_copy(
            src_ref=dests.at[s], dst_ref=dests.at[s],
            send_sem=dest_send.at[d], recv_sem=dest_recv.at[d],
            device_id=(lax.rem(s + d, n), t), device_id_type=MESH)

    @pl.loop(1, n)
    def _(d):
        dest_copy(d).start()

    for i, o in enumerate(OFFSETS):
        @pl.when(jnp.logical_not(has(-o)))
        def _():
            pairs[i + 1] = jnp.zeros(pairs.shape[1:], BF16)
            codes[i + 1] = jnp.zeros(codes.shape[1:], jnp.int32)

    index = merge_index[...] - s * count
    order = jnp.concatenate([index[j:j + 1] for j in range(tp)], axis=1)
    square = (count, count)
    down = lax.broadcasted_iota(jnp.int32, square, 0)
    along = lax.broadcasted_iota(jnp.int32, square, 1)
    diag = down == along
    order_column = jnp.sum(jnp.where(diag, order, 0), axis=1, keepdims=True)
    pick_all = (order_column == along).astype(BF16)
    picks[...] = pick_all

    def column(row):
        return jnp.sum(jnp.where(diag, row, 0), axis=1, keepdims=True)

    gain = first_gain[...].reshape(1, -1)
    gain_column = jnp.transpose(jnp.broadcast_to(gain, (128, gain.shape[1])))[:, 0:1]

    for i in range(2):
        tok_copy(i).wait_recv()
        tok_copy(i + 3).start()
    local[0].wait()
    tok_copy(2).wait_recv()
    for i in range(2):
        tok_copy(i + 3).wait_recv()
    packed = gathered[...].reshape(tp * width, count)
    residual = lax.dot_general(
        picks[pl.ds(pl.multiple_of(t * merged, merged), merged), :], packed,
        (((1,), (1,)), ((), ())), preferred_element_type=F32)
    normed = normalise(packed.astype(F32), gain_column, 0).astype(BF16)
    local[1].wait()
    pairs[0, 0:width] = jnp.dot(wk[...], normed, preferred_element_type=F32).astype(BF16)
    local[2].wait()
    pairs[0, width:2 * width] = jnp.dot(wv[...], normed, preferred_element_type=F32).astype(BF16)
    for i, o in enumerate(OFFSETS):
        @pl.when(has(o))
        def _():
            pair_copy(i).start()

    local[3].wait()
    queries[...] = jnp.dot(wq[...], normed, preferred_element_type=F32).astype(BF16)

    small = (merged, merged)
    first = lax.broadcasted_iota(jnp.int32, small, 0)
    second = lax.broadcasted_iota(jnp.int32, small, 1)

    def places(row):
        owner = jnp.floor(row.astype(F32) * (1.0 / merged))
        owner_column = jnp.sum(jnp.where(first == second, owner, 0.0), axis=1, keepdims=True)
        before = (owner_column == owner) & (first < second)
        return owner, jnp.sum(jnp.where(before, 1.0, 0.0), axis=0, keepdims=True)

    owner, rank = places(dests[s])
    block_row = lax.broadcasted_iota(jnp.int32, sort.shape, 0).astype(F32)
    sort[...] = (owner * BLOCK + rank == block_row).astype(BF16)
    in_block = lax.broadcasted_iota(jnp.int32, (BLOCK, merged), 0).astype(F32)

    def place(source):
        row = dests[source]
        owner, rank = places(row)
        here = ((owner == s.astype(F32)) & (rank == in_block)).astype(BF16)
        slots = ((row - s * merged) == first).astype(BF16)
        spread[source] = lax.dot_general(
            here, slots, (((1,), (1,)), ((), ())), preferred_element_type=F32).astype(BF16)

    place(s)

    @pl.loop(1, n)
    def _(d):
        dest_copy(d).wait_recv()
        place(lax.rem(s + n - d, n))

    factor = HD ** (-0.5) * LOG2E
    state = [None] * 4
    for b in range(5):
        if b:
            i = b - 1

            @pl.when(has(-OFFSETS[i]))
            def _():
                code_copy(i).wait_recv()
                pair_copy(i).wait_recv()
        allowed = column(codes[b]) == code_query
        if b == 0:
            allowed = allowed | diag
        for h in range(4):
            key = pairs[b, h * HD:(h + 1) * HD]
            value = pairs[b, width + h * HD:width + (h + 1) * HD]
            scores = lax.dot_general(
                key, queries[h * HD:(h + 1) * HD], (((0,), (0,)), ((), ())), preferred_element_type=F32)
            scores = jnp.where(allowed, scores * factor, -1e30)
            top = jnp.max(scores, axis=0, keepdims=True)
            if b:
                top = jnp.maximum(top, state[h][0])
            expo = jnp.exp2(scores - top)
            total = jnp.sum(expo, axis=0, keepdims=True)
            acc = jnp.dot(value, expo.astype(BF16), preferred_element_type=F32)
            if b:
                shrink = jnp.exp2(state[h][0] - top)
                total = total + shrink * state[h][1]
                acc = acc + shrink * state[h][2]
            state[h] = (top, total, acc)

    attended = jnp.concatenate([acc / total for _, total, acc in state], axis=0).astype(BF16)
    attended = lax.dot_general(
        picks[...], attended, (((1,), (1,)), ((), ())), preferred_element_type=F32).astype(BF16)
    local[4].wait()

    def part_copy(i):
        source = part_send.at[(far, beside, across)[i]]
        return pltpu.make_async_remote_copy(
            src_ref=source, dst_ref=part_recv.at[i], send_sem=part_ssem.at[i], recv_sem=part_rsem.at[i],
            device_id=(s, (beside, beside, across)[i]), device_id_type=MESH)

    part = jnp.dot(attended, wo[...], preferred_element_type=F32).astype(BF16)
    for j in range(tp):
        part_send[j] = part[j * merged:(j + 1) * merged]
    part_copy(0).start()
    part_copy(1).start()
    part_copy(0).wait_recv()
    part_send[across] = (part_send[across].astype(F32) + part_recv[0].astype(F32)).astype(BF16)
    part_copy(2).start()
    part_copy(1).wait_recv()
    updated = residual + part_send[t].astype(F32) + part_recv[1].astype(F32)
    part_copy(2).wait_recv()
    updated = updated + part_recv[2].astype(F32)
    merged_norm = normalise(updated, merge_gain[...].reshape(1, -1), 1).astype(BF16)
    local[5].wait()
    proj = jnp.dot(merged_norm, wm[...], preferred_element_type=F32)
    piece = proj.shape[1] // tp
    for j in range(tp):
        proj_send[j] = proj[:, j * piece:(j + 1) * piece].astype(BF16)

    def proj_copy(d):
        peer = lax.rem(t + d, tp)
        return pltpu.make_async_remote_copy(
            src_ref=proj_send.at[peer], dst_ref=proj_recv.at[d],
            send_sem=proj_ssem.at[d], recv_sem=proj_rsem.at[d],
            device_id=(s, peer), device_id_type=MESH)

    for d in range(1, tp):
        proj_copy(d).start()
    projected = proj_send[t].astype(F32)
    for d in range(1, tp):
        proj_copy(d).wait_recv()
        projected = projected + proj_recv[d].astype(F32)
    sorted_rows = jnp.dot(sort[...], projected.astype(BF16), preferred_element_type=F32).astype(BF16)
    leaving[...] = sorted_rows.reshape(leaving.shape)

    def row_copy(d):
        peer = lax.rem(s + d, n)
        return pltpu.make_async_remote_copy(
            src_ref=leaving.at[peer], dst_ref=rows.at[s],
            send_sem=row_send.at[d], recv_sem=row_recv.at[d],
            device_id=(peer, t), device_id_type=MESH)

    @pl.loop(1, n)
    def _(d):
        row_copy(d).start()

    rows[s] = leaving[s]

    @pl.loop(1, n)
    def _(d):
        row_copy(d).wait_recv()

    out[...] = lax.dot_general(
        spread[...].reshape(n * BLOCK, merged), rows[...].reshape(n * BLOCK, piece),
        (((0,), (0,)), ((), ())), preferred_element_type=F32).astype(BF16)

    for i in range(5):
        tok_copy(i).wait_send()
    for i in range(3):
        part_copy(i).wait_send()
    for d in range(1, tp):
        proj_copy(d).wait_send()
    for i, o in enumerate(OFFSETS):
        @pl.when(has(o))
        def _():
            code_copy(i).wait_send()
            pair_copy(i).wait_send()

    @pl.loop(1, n)
    def _(d):
        dest_copy(d).wait_send()
        row_copy(d).wait_send()


def body(n, tp, tokens, first_gain, w_query, w_key, w_value, w_out, segment_ids, keep_mask,
         merge_gain, w_merge, merge_index, destination):
    count, width = tokens.shape
    features = w_query.shape[0]
    merged = merge_index.shape[0]
    piece = w_merge.shape[1] // tp
    anywhere = pl.BlockSpec(memory_space=pl.ANY)
    vmem = pl.BlockSpec(memory_space=pltpu.VMEM)
    dma = pltpu.SemaphoreType.DMA
    return pl.pallas_call(
        functools.partial(kernel, n, tp),
        out_shape=jax.ShapeDtypeStruct((merged, piece), BF16),
        in_specs=[anywhere, vmem, anywhere, anywhere, anywhere, anywhere, vmem, vmem, vmem, anywhere, vmem, vmem],
        out_specs=vmem,
        scratch_shapes=[
            pltpu.VMEM((tp, width, count), BF16),
            pltpu.VMEM(w_query.shape[::-1], BF16),
            pltpu.VMEM(w_key.shape[::-1], BF16),
            pltpu.VMEM(w_value.shape[::-1], BF16),
            pltpu.VMEM(w_out.shape, BF16),
            pltpu.VMEM(w_merge.shape, BF16),
            pltpu.VMEM((5, 2 * width, count), BF16),
            pltpu.VMEM((5, 1, count), jnp.int32),
            pltpu.VMEM((n, 1, merged), jnp.int32),
            pltpu.VMEM((width, count), BF16),
            pltpu.VMEM((count, count), BF16),
            pltpu.VMEM((tp, merged, features), BF16),
            pltpu.VMEM((tp, merged, features), BF16),
            pltpu.VMEM((tp, merged, piece), BF16),
            pltpu.VMEM((tp, merged, piece), BF16),
            pltpu.VMEM((n * BLOCK, merged), BF16),
            pltpu.VMEM((n, BLOCK, merged), BF16),
            pltpu.VMEM((n, BLOCK, piece), BF16),
            pltpu.VMEM((n, BLOCK, piece), BF16),
            dma((6,)),
            dma((5,)), dma((5,)),
            dma((4,)), dma((4,)), dma((4,)), dma((4,)),
            dma((n,)), dma((n,)),
            dma((tp,)), dma((tp,)), dma((tp,)), dma((tp,)),
            dma((n,)), dma((n,)),
        ],
        compiler_params=pltpu.CompilerParams(
            collective_id=0, has_side_effects=True, vmem_limit_bytes=56 * 1024 * 1024),
        name="vision_layer",
    )(tokens.T, first_gain, w_query.T, w_key.T, w_value.T, w_out,
      segment_ids.reshape(1, -1), keep_mask.reshape(1, -1), merge_gain,
      w_merge, merge_index.T, destination.reshape(1, -1))


def solution(mesh):
    n, tp = mesh.shape["seq"], mesh.shape["tp"]
    return jax.shard_map(
        functools.partial(body, n, tp),
        mesh=mesh,
        in_specs=(
            P("seq", "tp"), P(), P(None, "tp"), P(None, "tp"), P(None, "tp"), P("tp", None),
            P("seq"), P("seq"), P(), P("tp", None), P("seq", None), P("seq"),
        ),
        out_specs=P("seq", "tp"),
        check_vma=False,
    )
```
